512 devices in a mesh: seq: 32 (over x, z), chan: 16 (over y, core).
Axes of the slice: x: 4, y: 8, z: 8, core: 2. Of those that a mesh axis runs over, the one named last changes fastest.
Arguments:
- query_gate: bfloat16 [16384, 8192], P('seq', 'chan'), may hold values from -23 to 23
- key_gate: bfloat16 [16384, 8192], P('seq', 'chan'), may hold values from -6 to 6
- value_input: bfloat16 [16384, 8192], P('seq', 'chan'), may hold values from -6 to 6
- filter_taps: bfloat16 [16384, 128], P('seq', 'chan'), may hold values from -1 to 1
- norm_gain: float32 [8192], P('chan'), may hold values from 0.5 to 1.5
Outputs:
- gated: bfloat16 [16384, 8192], P('seq', 'chan')
- normed: bfloat16 [16384, 8192], P('seq', 'chan')
The draws below stay inside these ranges and needn't reach their ends.
All inputs are finite; a program needn't handle non-finite values.
Results may differ from the reference program's by a relative error of at most 0.01.
Values may be sent and summed in bfloat16 or wider, within the bound.
A program may use at most 64 MiB of HBM per device.

```python
import math
import jax
import jax.numpy as jnp
from jax import lax

D = 8192
GROUPS = 128
TOK_DEV = 512
LENGTH = 16384
N_SEQ = 32


def draw_query_gate(key, part):
    base_key = jax.random.fold_in(key, 11)
    subkeys = jax.random.split(base_key, 3)
    channel_pos = jnp.arange(D, dtype=jnp.float32) / D
    channel_rough = jax.random.uniform(subkeys[1], (D,), dtype=jnp.float32)
    channel_scale = 10.0 ** (0.5 * channel_pos + 0.5 * channel_rough - 0.5)
    token_scale = 10.0 ** (0.5 * jax.random.uniform(subkeys[2], (LENGTH, 1), dtype=jnp.float32) - 0.25)
    values = jax.random.truncated_normal(subkeys[0], -4.0, 4.0, (LENGTH, D), dtype=jnp.float32)
    return (values * channel_scale[None, :] * token_scale).astype(jnp.bfloat16)


def draw_filter_taps(key, part):
    base_key = jax.random.fold_in(key, 23)
    subkeys = jax.random.split(base_key, 2)
    upper_log = math.log(4.0 * LENGTH)
    lower_log = math.log(32.0)
    decay_length = jnp.exp(jax.random.uniform(subkeys[1], (GROUPS,), dtype=jnp.float32, minval=lower_log, maxval=upper_log))
    positions = jnp.arange(LENGTH, dtype=jnp.float32)[:, None]
    envelope = jnp.exp(-positions / decay_length[None, :]) * jnp.sqrt(2.0 / decay_length)[None, :]
    noise = jax.random.truncated_normal(subkeys[0], -4.0, 4.0, (LENGTH, GROUPS), dtype=jnp.float32)
    return (noise * envelope).astype(jnp.bfloat16)


def block_scale(own_key, extent, cuts, smallest, top_value):
    factor_of, own = 1.0, jax.random.fold_in(own_key, 6)
    for dim, shards_of in cuts:
        steps = jnp.exp(jax.random.uniform(jax.random.fold_in(own, dim), (shards_of,), jnp.float32, smallest / len(cuts), top_value / len(cuts)))
        factor_of = factor_of * jnp.repeat(steps, extent[dim] // shards_of).reshape([-1 if axis == dim else 1 for axis in range(len(extent))])
    return factor_of


def gaussian(stream_key, dims, scale, most, cuts=(), kind=jnp.bfloat16):
    gain = block_scale(stream_key, dims, cuts, -0.22, 0.18) if cuts else 1.0
    drawn = jax.random.normal(stream_key, dims, jnp.float32) * scale * gain
    return jnp.minimum(jnp.maximum(drawn, -most), most).astype(kind)


def setup_inputs(seed: int = 0) -> dict:
    keys = jax.random.split(jax.random.key(seed), 6)
    query_gate = draw_query_gate(jax.random.fold_in(keys[5], 71), 0)
    key_gate = gaussian(keys[1], (LENGTH, D), 1.0, 6.0, ((0, 32), (1, 16)))
    value_input = gaussian(keys[2], (LENGTH, D), 1.0, 6.0, ((0, 32), (1, 16)))
    filter_taps = draw_filter_taps(jax.random.fold_in(keys[5], 71), 0)
    norm_gain = jnp.clip(1.0 + 0.1 * jax.random.normal(keys[4], (D,), jnp.float32), 0.5, 1.5)
    return {"query_gate": query_gate, "key_gate": key_gate, "value_input": value_input, "filter_taps": filter_taps, "norm_gain": norm_gain}


norm_eps = 1e-05

def angle_table(rows_count, cols_count, row_start, col_start, period):
    row_ids = row_start + lax.iota(jnp.int32, rows_count)
    col_ids = col_start + lax.iota(jnp.int32, cols_count)
    phases = row_ids[:, None] * col_ids[None, :] % period
    return phases.astype(jnp.float32) * (2.0 * math.pi / period)

def block_matrix(rows_count, cols_count, period):
    phases = angle_table(rows_count, cols_count, 0, 0, period)
    return jnp.stack([jnp.cos(phases), -jnp.sin(phases)]).astype(jnp.bfloat16)

def line_matrix(length, direction):
    phases = angle_table(length, length, 0, 0, length)
    cosine = jnp.cos(phases)
    sine_part = jnp.sin(phases) * direction
    upper = jnp.concatenate([cosine, sine_part], axis=1)
    lower = jnp.concatenate([-sine_part, cosine], axis=1)
    return jnp.concatenate([upper, lower], axis=0).astype(jnp.bfloat16)

def twiddle(halves, row_start, col_start, period, direction):
    phases = angle_table(halves.shape[1], halves.shape[2], row_start, col_start, period)
    cosine = jnp.cos(phases)[:, :, None]
    sine_part = direction * jnp.sin(phases)[:, :, None]
    real_part = halves[0] * cosine - halves[1] * sine_part
    imaginary = halves[1] * cosine + halves[0] * sine_part
    return jnp.stack([real_part, imaginary])

def blocks_forward(blocks_in, matrix):
    return jnp.einsum('abc,rak->rbkc', blocks_in.astype(jnp.float32), matrix.astype(jnp.float32))

def line_apply(halves, matrix):
    dims_all = halves.shape
    flattened = halves.reshape(2 * dims_all[1], dims_all[2] * dims_all[3])
    return jnp.dot(matrix, flattened, preferred_element_type=jnp.float32).reshape(dims_all)

def apply_filter(spectrum, filter_spec):
    dims_all = spectrum.shape
    group_count = filter_spec.shape[3]
    grouped = spectrum.reshape(dims_all[0], dims_all[1], dims_all[2], group_count, dims_all[3] // group_count)
    filter_real = filter_spec[0][..., None]
    filter_imaginary = filter_spec[1][..., None]
    real_part = grouped[0] * filter_real - grouped[1] * filter_imaginary
    imaginary = grouped[0] * filter_imaginary + grouped[1] * filter_real
    return jnp.stack([real_part, imaginary]).reshape(dims_all).astype(jnp.bfloat16)

def blocks_inverse(halves, matrix, factor):
    summed = jnp.einsum('rbkc,rka->abc', halves.astype(jnp.float32), matrix.astype(jnp.float32))
    return (summed * factor).astype(jnp.bfloat16)

def reference(query_gate, key_gate, value_input, filter_taps, norm_gain):
    blocks = N_SEQ
    tokens = TOK_DEV
    periods = 2 * LENGTH
    group_width = D // GROUPS
    product = (key_gate.astype(jnp.float32) * value_input.astype(jnp.float32)).astype(jnp.bfloat16)
    first_matrix = block_matrix(blocks, 2 * blocks, 2 * blocks)
    last_matrix = block_matrix(2 * blocks, blocks, 2 * blocks)
    line_forward = line_matrix(tokens, 1.0)
    line_backward = line_matrix(tokens, -1.0)

    def convolve(group):
        start = (group * group_width).astype(jnp.int32)
        data_rows = lax.dynamic_slice_in_dim(product, start, group_width, 1).reshape(blocks, tokens, group_width)
        taps_rows = lax.dynamic_slice_in_dim(filter_taps, group.astype(jnp.int32), 1, 1).reshape(blocks, tokens, 1)
        data_spread = twiddle(blocks_forward(data_rows, first_matrix), 0, 0, periods, -1.0).astype(jnp.bfloat16)
        taps_spread = twiddle(blocks_forward(taps_rows, first_matrix), 0, 0, periods, -1.0).astype(jnp.bfloat16)
        spectrum = line_apply(data_spread, line_forward)
        taps_spectrum = line_apply(taps_spread, line_forward)
        filtered = apply_filter(spectrum, taps_spectrum)
        returned = twiddle(line_apply(filtered, line_backward), 0, 0, periods, 1.0).astype(jnp.bfloat16)
        local_blocks = blocks_inverse(returned, last_matrix, 1.0 / periods)
        return local_blocks.reshape(LENGTH, group_width)
    pieces = lax.map(convolve, jnp.arange(GROUPS, dtype=jnp.int32))
    convolved = jnp.transpose(pieces, (1, 0, 2)).reshape(LENGTH, D)
    gated_full = query_gate.astype(jnp.float32) * convolved.astype(jnp.float32)
    mean_square = lax.optimization_barrier(jnp.mean(gated_full * gated_full, axis=1, keepdims=True))
    normed = gated_full * lax.rsqrt(mean_square + norm_eps) * norm_gain.astype(jnp.float32)[None, :]
    return (gated_full.astype(jnp.bfloat16), normed.astype(jnp.bfloat16))
```

```python
import functools

import jax
import jax.numpy as jnp
import ml_dtypes
import numpy as np
from jax import lax
from jax.experimental import pallas as pl
from jax.experimental.pallas import tpu as pltpu
from jax.sharding import PartitionSpec as P

D = 8192
GROUPS = 128
NORM_EPS = 1e-05
MESH = pl.DeviceIdType.MESH

X_DIM, Z_DIM = 4, 8
SEQ = X_DIM * Z_DIM
CHAN = 16
TOK = 512
CH = 512
CW = CH // SEQ
LINES = 2 * SEQ
HALF = LINES // 2 + 1
N = 2 * SEQ * TOK
FULL = LINES * CW
PARTS = 2
CP = CW // PARTS
BH = TOK // 2
ROWS = HALF * CP + CP
TPAD = 48


def rounded(values):
    return values.astype(np.float32).astype(ml_dtypes.bfloat16)


def constant_tables():
    k1 = np.arange(HALF)
    a = np.arange(SEQ)
    b = np.arange(TOK)
    ang = 2.0 * np.pi * ((k1[:, None] * a[None, :]) % LINES) / LINES
    cos_a, sin_a = np.cos(ang), np.sin(ang)
    eye = np.eye(CW)
    first = np.concatenate([cos_a, -sin_a[1:-1]], axis=0)
    first_kron = np.kron(first, eye)
    weight = np.full((HALF, 1), 2.0)
    weight[0] = weight[-1] = 1.0
    last = np.concatenate([weight * cos_a, -2.0 * sin_a[1:-1]], axis=0)
    last_kron = np.kron(last.T, eye)
    taps_first = np.zeros((2, TPAD, SEQ))
    taps_first[0, :HALF] = cos_a
    taps_first[1, 1 : HALF - 1] = -sin_a[1:-1]
    taps_first = taps_first.reshape(2 * TPAD, SEQ)
    tang = 2.0 * np.pi * ((k1[:, None] * b[None, :]) % N) / N
    twiddle = np.zeros((2, TPAD, TOK))
    twiddle[0, :HALF], twiddle[1, :HALF] = np.cos(tang), np.sin(tang)
    lang = 2.0 * np.pi * ((b[:, None] * b[None, :]) % TOK) / TOK
    c, s = np.cos(lang), np.sin(lang)
    forward = np.block([[c, -s], [s, c]])
    backward = np.block([[c, s], [-s, c]])
    order = np.concatenate(
        [np.concatenate([np.arange(128) + 128 * i, np.arange(128) + 128 * i + TOK]) for i in range(TOK // 128)]
    )
    forward = forward[:, order]
    backward = backward[order][:, order]
    pairs = np.concatenate([np.arange(256) + 256 * i for i in (0, 2, 1, 3)])
    backward = backward[:, pairs]
    return (
        rounded(first_kron),
        rounded(last_kron),
        rounded(taps_first),
        twiddle.astype(np.float32),
        rounded(forward),
        rounded(backward),
    )


def send_order():
    zs = (4, 3, 5, 2, 6, 1, 7, 0)
    out = []
    for k in range(Z_DIM):
        for dx in range(X_DIM):
            dz = zs[(k + 2 * dx) % Z_DIM]
            if (dx, dz) != (0, 0):
                out.append((dx, dz))
    return out


def kernel(
    q_hbm, k_hbm, v_hbm, taps_hbm, first_hbm, last_hbm, tfirst_hbm, twid_hbm, fwd_hbm, bwd_hbm,
    conv_ref, inverse_ref,
    q_ref, k_ref, v_ref, taps_ref, tfirst_ref, twid_ref,
    prod_t, data_in, taps_out, taps_in, taps_mat, taps_spec, q_t,
    first, last, fwd, bwd, spread, filtered, returned, back_out, back_in, conv, inverse_wide, sums_out, sums_in,
    load_sem, data_ssem, data_rsem, taps_ssem, taps_rsem, back_ssem, back_rsem, sum_ssem, sum_rsem,
):
    f32, bf16 = jnp.float32, jnp.bfloat16
    me = lax.axis_index("seq")
    ch = lax.axis_index("chan")
    my_x, my_z = me // Z_DIM, me % Z_DIM

    loads = [
        (k_hbm, k_ref), (v_hbm, v_ref), (taps_hbm, taps_ref), (q_hbm, q_ref), (tfirst_hbm, tfirst_ref),
        (twid_hbm, twid_ref), (fwd_hbm, fwd), (first_hbm, first), (bwd_hbm, bwd), (last_hbm, last),
    ]
    loads = [pltpu.make_async_copy(src, dst, load_sem.at[i]) for i, (src, dst) in enumerate(loads)]
    for load in loads:
        load.start()

    def peer(dx, dz):
        return lax.rem(my_x + dx, X_DIM) * Z_DIM + lax.rem(my_z + dz, Z_DIM)

    order = send_order()
    barrier = pltpu.get_barrier_semaphore()
    for dx, dz in order:
        pl.semaphore_signal(barrier, inc=1, device_id=(peer(dx, dz), ch), device_id_type=MESH)
    for d in range(1, CHAN):
        pl.semaphore_signal(barrier, inc=1, device_id=(me, lax.rem(ch + d, CHAN)), device_id_type=MESH)

    def block(j):
        return pl.ds(pl.multiple_of(j * CW, CW), CW)

    def channel_major(values, cb, dst):
        turned = jnp.transpose(values)
        for j in range(128 // CW):
            for h in range(PARTS):
                rows = slice(j * CW + h * CP, j * CW + h * CP + CP)
                both = jnp.concatenate([turned[rows, :BH], turned[rows, BH:]], axis=0)
                at = (cb * (128 // CW) + j) * CW
                dst[h, at : at + CW, :] = both.astype(bf16)

    loads[0].wait()
    loads[1].wait()
    for cb in range(CH // 128):
        lanes = slice(cb * 128, cb * 128 + 128)
        channel_major(k_ref[:, lanes].astype(f32) * v_ref[:, lanes].astype(f32), cb, prod_t)
    loads[2].wait()
    for g in range(8):
        taps_out[g] = taps_ref[g : g + 1, :].astype(f32)

    pl.semaphore_wait(barrier, SEQ - 1 + CHAN - 1)

    sends = []

    def exchange(src, dst, ssem, rsem):
        for dx, dz in order:
            j = peer(dx, dz)
            cp = pltpu.make_async_remote_copy(
                src.at[block(j)], dst.at[block(me)], ssem, rsem, device_id=(j, ch), device_id_type=MESH
            )
            cp.start()
            sends.append(cp)

    def arrived(dst, sem, count):
        pltpu.make_async_copy(dst.at[pl.ds(0, count)], dst.at[pl.ds(0, count)], sem).wait()

    exchange(prod_t.at[0], data_in.at[0], data_ssem.at[0], data_rsem.at[0])
    for dx, dz in order:
        j = peer(dx, dz)
        cp = pltpu.make_async_remote_copy(
            taps_out.at[j // 4], taps_in.at[me], taps_ssem, taps_rsem, device_id=(j, ch), device_id_type=MESH
        )
        cp.start()
        sends.append(cp)
    exchange(prod_t.at[1], data_in.at[1], data_ssem.at[1], data_rsem.at[1])
    taps_in[me] = taps_out[me // 4]
    for h in range(PARTS):
        data_in[h, block(me), :] = prod_t[h, block(me), :]

    loads[3].wait()
    for cb in range(CH // 128):
        lanes = slice(cb * 128, cb * 128 + 128)
        channel_major(q_ref[:, lanes].astype(f32), cb, q_t)

    for i in range(4, 8):
        loads[i].wait()
    arrived(taps_in, taps_rsem, SEQ - 1)
    for a in range(SEQ):
        taps_mat[a : a + 1, :] = taps_in[a]
    taps_y = jnp.dot(tfirst_ref[...], taps_mat[...].astype(bf16), preferred_element_type=f32)
    ty_re, ty_im = taps_y[:TPAD], taps_y[TPAD:]
    cos, sin = twid_ref[0], twid_ref[1]
    taps_spread = jnp.concatenate(
        [(ty_re * cos + ty_im * sin).astype(bf16), (ty_im * cos - ty_re * sin).astype(bf16)], axis=1
    )
    taps_spec[...] = jnp.dot(taps_spread, fwd[...], preferred_element_type=f32)
    loads[8].wait()
    loads[9].wait()

    zero = jnp.zeros((CP, BH), f32)

    def part(h):
        arrived(data_in.at[h], data_rsem.at[h], CH - CW)
        y = jnp.dot(first[...], data_in[h], preferred_element_type=f32)
        for bh in range(2):
            lanes = slice(bh * BH, bh * BH + BH)
            for m in range(ROWS // 16):
                res, ims = [], []
                for k1 in (2 * m, 2 * m + 1):
                    if k1 >= HALF:
                        res.append(zero)
                        ims.append(zero)
                        continue
                    at = k1 * CW + bh * CP
                    re = y[at : at + CP]
                    c = jnp.broadcast_to(twid_ref[0, k1 : k1 + 1, lanes], (CP, BH))
                    s = jnp.broadcast_to(twid_ref[1, k1 : k1 + 1, lanes], (CP, BH))
                    if 0 < k1 < HALF - 1:
                        at = (HALF + k1 - 1) * CW + bh * CP
                        im = y[at : at + CP]
                        res.append(re * c + im * s)
                        ims.append(im * c - re * s)
                    else:
                        res.append(re * c)
                        ims.append(-(re * s))
                rows = slice(m * 16, m * 16 + 16)
                spread[h, rows, lanes] = jnp.concatenate(res, axis=0).astype(bf16)
                spread[h, rows, slice(TOK + bh * BH, TOK + bh * BH + BH)] = jnp.concatenate(ims, axis=0).astype(bf16)

        for nb in range(TOK // 128):
            sp = jnp.dot(spread[h], fwd[:, nb * 256 : nb * 256 + 256], preferred_element_type=f32)
            lr, li = slice(nb * 256, nb * 256 + 128), slice(nb * 256 + 128, nb * 256 + 256)
            for m in range(ROWS // 16):
                res, ims = [], []
                for k1 in (2 * m, 2 * m + 1):
                    hr = jnp.broadcast_to(taps_spec[k1 : k1 + 1, lr], (CP, 128))
                    hi = jnp.broadcast_to(taps_spec[k1 : k1 + 1, li], (CP, 128))
                    rows = slice(k1 * CP, k1 * CP + CP)
                    sr, si = sp[rows, :128], sp[rows, 128:]
                    res.append(sr * hr - si * hi)
                    ims.append(sr * hi + si * hr)
                rows = slice(m * 16, m * 16 + 16)
                filtered[h, rows, lr] = jnp.concatenate(res, axis=0).astype(bf16)
                filtered[h, rows, li] = jnp.concatenate(ims, axis=0).astype(bf16)

        for nb in range(BH // 128):
            inv = jnp.dot(filtered[h], bwd[:, nb * 512 : nb * 512 + 512], preferred_element_type=f32)
            for k1 in range(HALF):
                rows = slice(k1 * CP, k1 * CP + CP)
                res, ims = [], []
                for bh in range(2):
                    lanes = slice(bh * BH + nb * 128, bh * BH + nb * 128 + 128)
                    c = jnp.broadcast_to(twid_ref[0, k1 : k1 + 1, lanes], (CP, 128))
                    s = jnp.broadcast_to(twid_ref[1, k1 : k1 + 1, lanes], (CP, 128))
                    re = inv[rows, bh * 256 : bh * 256 + 128]
                    im = inv[rows, bh * 256 + 128 : bh * 256 + 256]
                    res.append(re * c - im * s)
                    ims.append(im * c + re * s)
                lanes = slice(nb * 128, nb * 128 + 128)
                returned[h, k1 * CW : k1 * CW + CW, lanes] = jnp.concatenate(res, axis=0).astype(bf16)
                if 0 < k1 < HALF - 1:
                    at = (HALF + k1 - 1) * CW
                    returned[h, at : at + CW, lanes] = jnp.concatenate(ims, axis=0).astype(bf16)

        z = jnp.dot(last[...], returned[h], preferred_element_type=f32)
        back_out[h] = (z * (1.0 / N)).astype(bf16)
        exchange(back_out.at[h], back_in.at[h], back_ssem.at[h], back_rsem.at[h])
        back_in[h, block(me), :] = back_out[h, block(me), :]

    for h in range(PARTS):
        part(h)

    totals = [jnp.zeros((CP, BH), f32), jnp.zeros((CP, BH), f32)]
    for h in range(PARTS):
        arrived(back_in.at[h], back_rsem.at[h], CH - CW)
        for j in range(SEQ):
            rows = slice(j * CW, j * CW + CW)
            g = q_t[h, rows, :].astype(f32) * back_in[h, rows, :].astype(f32)
            g = g * g
            totals = [totals[0] + g[:CP], totals[1] + g[CP:]]
    for bh in range(2):
        sums_out[:, bh * BH : bh * BH + BH] = jnp.sum(totals[bh], axis=0, keepdims=True)
    for d in range(1, CHAN):
        cp = pltpu.make_async_remote_copy(
            sums_out, sums_in.at[ch], sum_ssem, sum_rsem, device_id=(me, lax.rem(ch + d, CHAN)), device_id_type=MESH
        )
        cp.start()
        sends.append(cp)
    sums_in[ch] = sums_out[...]

    for cb in range(CH // 128):
        rows = []
        for j in range(128 // CW):
            at = (cb * (128 // CW) + j) * CW
            for h in range(PARTS):
                tile = back_in[h, at : at + CW, :].astype(f32)
                rows.append(jnp.concatenate([tile[:CP], tile[CP:]], axis=1))
        conv[:, cb * 128 : cb * 128 + 128] = jnp.transpose(jnp.concatenate(rows, axis=0)).astype(bf16)
    conv_store = pltpu.make_async_copy(conv, conv_ref, load_sem.at[0])
    conv_store.start()

    arrived(sums_in, sum_rsem, CHAN - 1)
    square = sums_in[0]
    for i in range(1, CHAN):
        square = square + sums_in[i]
    inverse = lax.rsqrt(square / D + NORM_EPS)
    inverse_wide[...] = jnp.transpose(jnp.broadcast_to(inverse, (128, TOK)))
    inverse_store = pltpu.make_async_copy(inverse_wide, inverse_ref, load_sem.at[1])
    inverse_store.start()
    for cp in sends:
        cp.wait_send()
    conv_store.wait()
    inverse_store.wait()


def gate_and_norm(q_ref, conv_ref, inverse_ref, gain_ref, gated_ref, normed_ref):
    f32, bf16 = jnp.float32, jnp.bfloat16
    inverse = inverse_ref[...]
    for cb in range(CH // 128):
        lanes = slice(cb * 128, cb * 128 + 128)
        g = q_ref[:, lanes].astype(f32) * conv_ref[:, lanes].astype(f32)
        gated_ref[:, lanes] = g.astype(bf16)
        normed_ref[:, lanes] = (g * inverse * gain_ref[:, lanes]).astype(bf16)


def body(query_gate, key_gate, value_input, filter_taps, norm_gain):
    bf16, f32 = jnp.bfloat16, jnp.float32
    tables = [jnp.asarray(t) for t in constant_tables()]
    hbm = pl.BlockSpec(memory_space=pltpu.HBM)
    dma = pltpu.SemaphoreType.DMA
    conv, inverse = pl.pallas_call(
        kernel,
        out_shape=[jax.ShapeDtypeStruct((TOK, CH), bf16), jax.ShapeDtypeStruct((TOK, 128), f32)],
        in_specs=[hbm] * 10,
        out_specs=[hbm, hbm],
        scratch_shapes=[
            pltpu.VMEM((TOK, CH), bf16),
            pltpu.VMEM((TOK, CH), bf16),
            pltpu.VMEM((TOK, CH), bf16),
            pltpu.VMEM((8, TOK), bf16),
            pltpu.VMEM((2 * TPAD, SEQ), bf16),
            pltpu.VMEM((2, TPAD, TOK), f32),
            pltpu.VMEM((PARTS, CH, BH), bf16),
            pltpu.VMEM((PARTS, CH, BH), bf16),
            pltpu.VMEM((8, 1, TOK), f32),
            pltpu.VMEM((SEQ, 1, TOK), f32),
            pltpu.VMEM((SEQ, TOK), f32),
            pltpu.VMEM((TPAD, 2 * TOK), f32),
            pltpu.VMEM((PARTS, CH, BH), bf16),
            pltpu.VMEM((FULL, CH), bf16),
            pltpu.VMEM((CH, FULL), bf16),
            pltpu.VMEM((2 * TOK, 2 * TOK), bf16),
            pltpu.VMEM((2 * TOK, 2 * TOK), bf16),
            pltpu.VMEM((PARTS, ROWS, 2 * TOK), bf16),
            pltpu.VMEM((PARTS, ROWS, 2 * TOK), bf16),
            pltpu.VMEM((PARTS, FULL, BH), bf16),
            pltpu.VMEM((PARTS, CH, BH), bf16),
            pltpu.VMEM((PARTS, CH, BH), bf16),
            pltpu.VMEM((TOK, CH), bf16),
            pltpu.VMEM((TOK, 128), f32),
            pltpu.VMEM((1, TOK), f32),
            pltpu.VMEM((CHAN, 1, TOK), f32),
            dma((10,)), dma((PARTS,)), dma((PARTS,)), dma, dma, dma((PARTS,)), dma((PARTS,)), dma, dma,
        ],
        compiler_params=pltpu.CompilerParams(
            collective_id=0, has_side_effects=True, vmem_limit_bytes=56 * 1024 * 1024
        ),
    )(query_gate, key_gate, value_input, jnp.transpose(filter_taps), *tables)
    steps = 2
    wide = pl.BlockSpec((TOK // steps, CH), lambda i: (i, 0))
    return pl.pallas_call(
        gate_and_norm,
        grid=(steps,),
        out_shape=[jax.ShapeDtypeStruct((TOK, CH), bf16)] * 2,
        in_specs=[
            wide, wide, pl.BlockSpec((TOK // steps, 128), lambda i: (i, 0)), pl.BlockSpec((1, CH), lambda i: (0, 0))
        ],
        out_specs=[wide, wide],
        compiler_params=pltpu.CompilerParams(vmem_limit_bytes=56 * 1024 * 1024),
    )(query_gate, conv, inverse, norm_gain.reshape(1, CH))


def solution(mesh):
    placed = (P("seq", "chan"), P("seq", "chan"), P("seq", "chan"), P("seq", "chan"), P("chan"))
    return jax.shard_map(
        body,
        mesh=mesh,
        in_specs=placed,
        out_specs=(P("seq", "chan"), P("seq", "chan")),
        check_vma=False,
    )
```

```python
import functools

import jax
import jax.numpy as jnp
import ml_dtypes
import numpy as np
from jax import lax
from jax.experimental import pallas as pl
from jax.experimental.pallas import tpu as pltpu
from jax.sharding import PartitionSpec as P

D = 8192
GROUPS = 128
NORM_EPS = 1e-05
MESH = pl.DeviceIdType.MESH

X_DIM, Z_DIM = 4, 8
SEQ = X_DIM * Z_DIM
CHAN = 16
TOK = 512
CH = 512
CW = CH // SEQ
LINES = 2 * SEQ
HALF = LINES // 2 + 1
N = 2 * SEQ * TOK
FULL = LINES * CW
PARTS = 2
CP = CW // PARTS
BH = TOK // 2
ROWS = HALF * CP + CP
TPAD = 48


def rounded(values):
    return values.astype(np.float32).astype(ml_dtypes.bfloat16)


def constant_tables():
    k1 = np.arange(HALF)
    a = np.arange(SEQ)
    b = np.arange(TOK)
    ang = 2.0 * np.pi * ((k1[:, None] * a[None, :]) % LINES) / LINES
    cos_a, sin_a = np.cos(ang), np.sin(ang)
    eye = np.eye(CW)
    first = np.concatenate([cos_a, -sin_a[1:-1]], axis=0)
    first_kron = np.kron(first, eye)
    weight = np.full((HALF, 1), 2.0)
    weight[0] = weight[-1] = 1.0
    last = np.concatenate([weight * cos_a, -2.0 * sin_a[1:-1]], axis=0)
    last_kron = np.kron(last.T, eye)
    taps_first = np.zeros((2, TPAD, SEQ))
    taps_first[0, :HALF] = cos_a
    taps_first[1, 1 : HALF - 1] = -sin_a[1:-1]
    taps_first = taps_first.reshape(2 * TPAD, SEQ)
    tang = 2.0 * np.pi * ((k1[:, None] * b[None, :]) % N) / N
    twiddle = np.zeros((2, TPAD, TOK))
    twiddle[0, :HALF], twiddle[1, :HALF] = np.cos(tang), np.sin(tang)
    lang = 2.0 * np.pi * ((b[:, None] * b[None, :]) % TOK) / TOK
    c, s = np.cos(lang), np.sin(lang)
    forward = np.block([[c, -s], [s, c]])
    backward = np.block([[c, s], [-s, c]])
    order = np.concatenate(
        [np.concatenate([np.arange(128) + 128 * i, np.arange(128) + 128 * i + TOK]) for i in range(TOK // 128)]
    )
    forward = forward[:, order]
    backward = backward[order][:, order]
    pairs = np.concatenate([np.arange(256) + 256 * i for i in (0, 2, 1, 3)])
    backward = backward[:, pairs]
    return (
        rounded(first_kron),
        rounded(last_kron),
        rounded(taps_first),
        twiddle.astype(np.float32),
        rounded(forward),
        rounded(backward),
    )


def send_order():
    out = []
    for dx in (1, 3, 2, 0):
        for dz in (4, 3, 5, 2, 6, 1, 7, 0):
            if (dx, dz) != (0, 0):
                out.append((dx, dz))
    return out


def kernel(
    q_hbm, k_hbm, v_hbm, taps_hbm, first_hbm, last_hbm, tfirst_hbm, twid_hbm, fwd_hbm, bwd_hbm,
    conv_ref, inverse_ref,
    q_ref, k_ref, v_ref, taps_ref, tfirst_ref, twid_ref,
    prod_t, data_in, taps_out, taps_in, taps_mat, taps_spec, q_t,
    first, last, fwd, bwd, spread, filtered, returned, back_out, back_in, sums_out, sums_in,
    load_sem, data_ssem, data_rsem, taps_ssem, taps_rsem, back_ssem, back_rsem, sum_ssem, sum_rsem,
):
    f32, bf16 = jnp.float32, jnp.bfloat16
    me = lax.axis_index("seq")
    ch = lax.axis_index("chan")
    my_x, my_z = me // Z_DIM, me % Z_DIM

    loads = [
        (k_hbm, k_ref), (v_hbm, v_ref), (taps_hbm, taps_ref), (q_hbm, q_ref), (tfirst_hbm, tfirst_ref),
        (twid_hbm, twid_ref), (fwd_hbm, fwd), (first_hbm, first), (bwd_hbm, bwd), (last_hbm, last),
    ]
    loads = [pltpu.make_async_copy(src, dst, load_sem.at[i]) for i, (src, dst) in enumerate(loads)]
    for load in loads:
        load.start()

    def peer(dx, dz):
        return lax.rem(my_x + dx, X_DIM) * Z_DIM + lax.rem(my_z + dz, Z_DIM)

    order = send_order()
    barrier = pltpu.get_barrier_semaphore()
    for dx, dz in order:
        pl.semaphore_signal(barrier, inc=1, device_id=(peer(dx, dz), ch), device_id_type=MESH)
    for d in range(1, CHAN):
        pl.semaphore_signal(barrier, inc=1, device_id=(me, lax.rem(ch + d, CHAN)), device_id_type=MESH)

    def block(j):
        return pl.ds(pl.multiple_of(j * CW, CW), CW)

    def channel_major(values, cb, dst):
        turned = jnp.transpose(values)
        for j in range(128 // CW):
            for h in range(PARTS):
                rows = slice(j * CW + h * CP, j * CW + h * CP + CP)
                both = jnp.concatenate([turned[rows, :BH], turned[rows, BH:]], axis=0)
                at = (cb * (128 // CW) + j) * CW
                dst[h, at : at + CW, :] = both.astype(bf16)

    loads[0].wait()
    loads[1].wait()
    for cb in range(CH // 128):
        lanes = slice(cb * 128, cb * 128 + 128)
        channel_major(k_ref[:, lanes].astype(f32) * v_ref[:, lanes].astype(f32), cb, prod_t)
    loads[2].wait()
    for g in range(8):
        taps_out[g] = taps_ref[g : g + 1, :].astype(f32)

    pl.semaphore_wait(barrier, SEQ - 1 + CHAN - 1)

    sends = []

    def exchange(src, dst, ssem, rsem):
        for dx, dz in order:
            j = peer(dx, dz)
            cp = pltpu.make_async_remote_copy(
                src.at[block(j)], dst.at[block(me)], ssem, rsem, device_id=(j, ch), device_id_type=MESH
            )
            cp.start()
            sends.append(cp)

    def arrived(dst, sem, count):
        pltpu.make_async_copy(dst.at[pl.ds(0, count)], dst.at[pl.ds(0, count)], sem).wait()

    exchange(prod_t.at[0], data_in.at[0], data_ssem.at[0], data_rsem.at[0])
    for dx, dz in order:
        j = peer(dx, dz)
        cp = pltpu.make_async_remote_copy(
            taps_out.at[j // 4], taps_in.at[me], taps_ssem, taps_rsem, device_id=(j, ch), device_id_type=MESH
        )
        cp.start()
        sends.append(cp)
    exchange(prod_t.at[1], data_in.at[1], data_ssem.at[1], data_rsem.at[1])
    taps_in[me] = taps_out[me // 4]
    for h in range(PARTS):
        data_in[h, block(me), :] = prod_t[h, block(me), :]

    loads[3].wait()
    for cb in range(CH // 128):
        lanes = slice(cb * 128, cb * 128 + 128)
        channel_major(q_ref[:, lanes].astype(f32), cb, q_t)

    for i in range(4, 8):
        loads[i].wait()
    arrived(taps_in, taps_rsem, SEQ - 1)
    for a in range(SEQ):
        taps_mat[a : a + 1, :] = taps_in[a]
    taps_y = jnp.dot(tfirst_ref[...], taps_mat[...].astype(bf16), preferred_element_type=f32)
    ty_re, ty_im = taps_y[:TPAD], taps_y[TPAD:]
    cos, sin = twid_ref[0], twid_ref[1]
    taps_spread = jnp.concatenate(
        [(ty_re * cos + ty_im * sin).astype(bf16), (ty_im * cos - ty_re * sin).astype(bf16)], axis=1
    )
    taps_spec[...] = jnp.dot(taps_spread, fwd[...], preferred_element_type=f32)
    loads[8].wait()
    loads[9].wait()

    zero = jnp.zeros((CP, BH), f32)

    def part(h):
        arrived(data_in.at[h], data_rsem.at[h], CH - CW)
        y = jnp.dot(first[...], data_in[h], preferred_element_type=f32)
        for bh in range(2):
            lanes = slice(bh * BH, bh * BH + BH)
            for m in range(ROWS // 16):
                res, ims = [], []
                for k1 in (2 * m, 2 * m + 1):
                    if k1 >= HALF:
                        res.append(zero)
                        ims.append(zero)
                        continue
                    at = k1 * CW + bh * CP
                    re = y[at : at + CP]
                    c = jnp.broadcast_to(twid_ref[0, k1 : k1 + 1, lanes], (CP, BH))
                    s = jnp.broadcast_to(twid_ref[1, k1 : k1 + 1, lanes], (CP, BH))
                    if 0 < k1 < HALF - 1:
                        at = (HALF + k1 - 1) * CW + bh * CP
                        im = y[at : at + CP]
                        res.append(re * c + im * s)
                        ims.append(im * c - re * s)
                    else:
                        res.append(re * c)
                        ims.append(-(re * s))
                rows = slice(m * 16, m * 16 + 16)
                spread[h, rows, lanes] = jnp.concatenate(res, axis=0).astype(bf16)
                spread[h, rows, slice(TOK + bh * BH, TOK + bh * BH + BH)] = jnp.concatenate(ims, axis=0).astype(bf16)

        for nb in range(TOK // 128):
            sp = jnp.dot(spread[h], fwd[:, nb * 256 : nb * 256 + 256], preferred_element_type=f32)
            lr, li = slice(nb * 256, nb * 256 + 128), slice(nb * 256 + 128, nb * 256 + 256)
            for m in range(ROWS // 16):
                res, ims = [], []
                for k1 in (2 * m, 2 * m + 1):
                    hr = jnp.broadcast_to(taps_spec[k1 : k1 + 1, lr], (CP, 128))
                    hi = jnp.broadcast_to(taps_spec[k1 : k1 + 1, li], (CP, 128))
                    rows = slice(k1 * CP, k1 * CP + CP)
                    sr, si = sp[rows, :128], sp[rows, 128:]
                    res.append(sr * hr - si * hi)
                    ims.append(sr * hi + si * hr)
                rows = slice(m * 16, m * 16 + 16)
                filtered[h, rows, lr] = jnp.concatenate(res, axis=0).astype(bf16)
                filtered[h, rows, li] = jnp.concatenate(ims, axis=0).astype(bf16)

        for nb in range(BH // 128):
            inv = jnp.dot(filtered[h], bwd[:, nb * 512 : nb * 512 + 512], preferred_element_type=f32)
            for k1 in range(HALF):
                rows = slice(k1 * CP, k1 * CP + CP)
                res, ims = [], []
                for bh in range(2):
                    lanes = slice(bh * BH + nb * 128, bh * BH + nb * 128 + 128)
                    c = jnp.broadcast_to(twid_ref[0, k1 : k1 + 1, lanes], (CP, 128))
                    s = jnp.broadcast_to(twid_ref[1, k1 : k1 + 1, lanes], (CP, 128))
                    re = inv[rows, bh * 256 : bh * 256 + 128]
                    im = inv[rows, bh * 256 + 128 : bh * 256 + 256]
                    res.append(re * c - im * s)
                    ims.append(im * c + re * s)
                lanes = slice(nb * 128, nb * 128 + 128)
                returned[h, k1 * CW : k1 * CW + CW, lanes] = jnp.concatenate(res, axis=0).astype(bf16)
                if 0 < k1 < HALF - 1:
                    at = (HALF + k1 - 1) * CW
                    returned[h, at : at + CW, lanes] = jnp.concatenate(ims, axis=0).astype(bf16)

        z = jnp.dot(last[...], returned[h], preferred_element_type=f32)
        back_out[h] = (z * (1.0 / N)).astype(bf16)
        exchange(back_out.at[h], back_in.at[h], back_ssem.at[h], back_rsem.at[h])
        back_in[h, block(me), :] = back_out[h, block(me), :]

    for h in range(PARTS):
        part(h)

    totals = [jnp.zeros((CP, BH), f32), jnp.zeros((CP, BH), f32)]
    for h in range(PARTS):
        arrived(back_in.at[h], back_rsem.at[h], CH - CW)
        for j in range(SEQ):
            rows = slice(j * CW, j * CW + CW)
            g = q_t[h, rows, :].astype(f32) * back_in[h, rows, :].astype(f32)
            g = g * g
            totals = [totals[0] + g[:CP], totals[1] + g[CP:]]
    for bh in range(2):
        sums_out[:, bh * BH : bh * BH + BH] = jnp.sum(totals[bh], axis=0, keepdims=True)
    for d in range(1, CHAN):
        cp = pltpu.make_async_remote_copy(
            sums_out, sums_in.at[ch], sum_ssem, sum_rsem, device_id=(me, lax.rem(ch + d, CHAN)), device_id_type=MESH
        )
        cp.start()
        sends.append(cp)
    sums_in[ch] = sums_out[...]

    for cb in range(CH // 128):
        rows = []
        for j in range(128 // CW):
            at = (cb * (128 // CW) + j) * CW
            for h in range(PARTS):
                tile = back_in[h, at : at + CW, :].astype(f32)
                rows.append(jnp.concatenate([tile[:CP], tile[CP:]], axis=1))
        conv_ref[:, cb * 128 : cb * 128 + 128] = jnp.transpose(jnp.concatenate(rows, axis=0)).astype(bf16)

    arrived(sums_in, sum_rsem, CHAN - 1)
    square = sums_in[0]
    for i in range(1, CHAN):
        square = square + sums_in[i]
    inverse = lax.rsqrt(square / D + NORM_EPS)
    inverse_ref[...] = jnp.transpose(jnp.broadcast_to(inverse, (128, TOK)))
    for cp in sends:
        cp.wait_send()


def gate_and_norm(q_ref, conv_ref, inverse_ref, gain_ref, gated_ref, normed_ref):
    f32, bf16 = jnp.float32, jnp.bfloat16
    tokens = gated_ref.shape[0]
    rows = pl.ds(pl.multiple_of(pl.program_id(0) * tokens, tokens), tokens)
    inverse = inverse_ref[rows, :]
    for cb in range(CH // 128):
        lanes = slice(cb * 128, cb * 128 + 128)
        g = q_ref[rows, lanes].astype(f32) * conv_ref[rows, lanes].astype(f32)
        gated_ref[:, lanes] = g.astype(bf16)
        normed_ref[:, lanes] = (g * inverse * gain_ref[:, lanes]).astype(bf16)


def body(query_gate, key_gate, value_input, filter_taps, norm_gain):
    bf16, f32 = jnp.bfloat16, jnp.float32
    tables = [jnp.asarray(t) for t in constant_tables()]
    hbm = pl.BlockSpec(memory_space=pltpu.HBM)
    dma = pltpu.SemaphoreType.DMA
    operands = [query_gate, key_gate, value_input, jnp.transpose(filter_taps), *tables]
    vmem = pl.BlockSpec(memory_space=pltpu.VMEM)
    conv, inverse = pl.pallas_call(
        kernel,
        out_shape=[pltpu.VMEM((TOK, CH), bf16), pltpu.VMEM((TOK, 128), f32)],
        in_specs=[hbm] * 10,
        out_specs=[vmem, vmem],
        scratch_shapes=[
            pltpu.VMEM((TOK, CH), bf16),
            pltpu.VMEM((TOK, CH), bf16),
            pltpu.VMEM((TOK, CH), bf16),
            pltpu.VMEM((8, TOK), bf16),
            pltpu.VMEM((2 * TPAD, SEQ), bf16),
            pltpu.VMEM((2, TPAD, TOK), f32),
            pltpu.VMEM((PARTS, CH, BH), bf16),
            pltpu.VMEM((PARTS, CH, BH), bf16),
            pltpu.VMEM((8, 1, TOK), f32),
            pltpu.VMEM((SEQ, 1, TOK), f32),
            pltpu.VMEM((SEQ, TOK), f32),
            pltpu.VMEM((TPAD, 2 * TOK), f32),
            pltpu.VMEM((PARTS, CH, BH), bf16),
            pltpu.VMEM((FULL, CH), bf16),
            pltpu.VMEM((CH, FULL), bf16),
            pltpu.VMEM((2 * TOK, 2 * TOK), bf16),
            pltpu.VMEM((2 * TOK, 2 * TOK), bf16),
            pltpu.VMEM((PARTS, ROWS, 2 * TOK), bf16),
            pltpu.VMEM((PARTS, ROWS, 2 * TOK), bf16),
            pltpu.VMEM((PARTS, FULL, BH), bf16),
            pltpu.VMEM((PARTS, CH, BH), bf16),
            pltpu.VMEM((PARTS, CH, BH), bf16),
            pltpu.VMEM((1, TOK), f32),
            pltpu.VMEM((CHAN, 1, TOK), f32),
            dma((10,)), dma((PARTS,)), dma((PARTS,)), dma, dma, dma((PARTS,)), dma((PARTS,)), dma, dma,
        ],
        compiler_params=pltpu.CompilerParams(
            collective_id=0, has_side_effects=True, vmem_limit_bytes=48 * 1024 * 1024
        ),
    )(*[pltpu.with_memory_space_constraint(x, pltpu.HBM) for x in operands])
    steps = 4
    wide = pl.BlockSpec((TOK // steps, CH), lambda i: (i, 0))
    return pl.pallas_call(
        gate_and_norm,
        grid=(steps,),
        out_shape=[jax.ShapeDtypeStruct((TOK, CH), bf16)] * 2,
        in_specs=[vmem] * 4,
        out_specs=[wide, wide],
        compiler_params=pltpu.CompilerParams(vmem_limit_bytes=32 * 1024 * 1024),
    )(query_gate, conv, inverse, norm_gain.reshape(1, CH))


def solution(mesh):
    placed = (P("seq", "chan"), P("seq", "chan"), P("seq", "chan"), P("seq", "chan"), P("chan"))
    return jax.shard_map(
        body,
        mesh=mesh,
        in_specs=placed,
        out_specs=(P("seq", "chan"), P("seq", "chan")),
        check_vma=False,
    )
```

```python
import functools

import jax
import jax.numpy as jnp
import ml_dtypes
import numpy as np
from jax import lax
from jax.experimental import pallas as pl
from jax.experimental.pallas import tpu as pltpu
from jax.sharding import PartitionSpec as P

D = 8192
GROUPS = 128
NORM_EPS = 1e-05
MESH = pl.DeviceIdType.MESH

X_DIM, Z_DIM = 4, 8
SEQ = X_DIM * Z_DIM
CHAN = 16
TOK = 512
CH = 512
CW = CH // SEQ
LINES = 2 * SEQ
HALF = LINES // 2 + 1
N = 2 * SEQ * TOK
FULL = LINES * CW
PARTS = 2
CP = CW // PARTS
BH = TOK // 2
ROWS = HALF * CP + CP
TPAD = 48


def rounded(values):
    return values.astype(np.float32).astype(ml_dtypes.bfloat16)


def constant_tables():
    k1 = np.arange(HALF)
    a = np.arange(SEQ)
    b = np.arange(TOK)
    ang = 2.0 * np.pi * ((k1[:, None] * a[None, :]) % LINES) / LINES
    cos_a, sin_a = np.cos(ang), np.sin(ang)
    eye = np.eye(CW)
    first = np.concatenate([cos_a, -sin_a[1:-1]], axis=0)
    first_kron = np.kron(first, eye)
    weight = np.full((HALF, 1), 2.0)
    weight[0] = weight[-1] = 1.0
    last = np.concatenate([weight * cos_a, -2.0 * sin_a[1:-1]], axis=0)
    last_kron = np.kron(last.T, eye)
    taps_first = np.zeros((2, TPAD, SEQ))
    taps_first[0, :HALF] = cos_a
    taps_first[1, 1 : HALF - 1] = -sin_a[1:-1]
    taps_first = taps_first.reshape(2 * TPAD, SEQ)
    tang = 2.0 * np.pi * ((k1[:, None] * b[None, :]) % N) / N
    twiddle = np.zeros((2, TPAD, TOK))
    twiddle[0, :HALF], twiddle[1, :HALF] = np.cos(tang), np.sin(tang)
    lang = 2.0 * np.pi * ((b[:, None] * b[None, :]) % TOK) / TOK
    c, s = np.cos(lang), np.sin(lang)
    forward = np.block([[c, -s], [s, c]])
    backward = np.block([[c, s], [-s, c]])
    order = np.concatenate(
        [np.concatenate([np.arange(128) + 128 * i, np.arange(128) + 128 * i + TOK]) for i in range(TOK // 128)]
    )
    forward = forward[:, order]
    backward = backward[order][:, order]
    pairs = np.concatenate([np.arange(256) + 256 * i for i in (0, 2, 1, 3)])
    backward = backward[:, pairs]
    return (
        rounded(first_kron),
        rounded(last_kron),
        rounded(taps_first),
        twiddle.astype(np.float32),
        rounded(forward),
        rounded(backward),
    )


def send_order():
    out = []
    for dx in (2, 1, 3, 0):
        for dz in (4, 1, 5, 2, 6, 3, 7, 0):
            if (dx, dz) != (0, 0):
                out.append((dx, dz))
    return out


def kernel(
    q_hbm, k_hbm, v_hbm, taps_hbm, first_hbm, last_hbm, tfirst_hbm, twid_hbm, fwd_hbm, bwd_hbm,
    conv_ref, inverse_ref,
    q_ref, k_ref, v_ref, taps_ref, tfirst_ref, twid_ref,
    prod_t, data_in, taps_out, taps_in, taps_mat, taps_spec, q_t,
    first, last, fwd, bwd, spread, filtered, returned, back_out, back_in, sums_out, sums_in,
    load_sem, data_ssem, data_rsem, taps_ssem, taps_rsem, back_ssem, back_rsem, sum_ssem, sum_rsem,
):
    f32, bf16 = jnp.float32, jnp.bfloat16
    me = lax.axis_index("seq")
    ch = lax.axis_index("chan")
    my_x, my_z = me // Z_DIM, me % Z_DIM

    loads = [
        (k_hbm, k_ref), (v_hbm, v_ref), (taps_hbm, taps_ref), (q_hbm, q_ref), (tfirst_hbm, tfirst_ref),
        (twid_hbm, twid_ref), (fwd_hbm, fwd), (first_hbm, first), (bwd_hbm, bwd), (last_hbm, last),
    ]
    loads = [pltpu.make_async_copy(src, dst, load_sem.at[i]) for i, (src, dst) in enumerate(loads)]
    for load in loads[:3]:
        load.start()

    def peer(dx, dz):
        return lax.rem(my_x + dx, X_DIM) * Z_DIM + lax.rem(my_z + dz, Z_DIM)

    order = send_order()
    far_first = sorted(range(1, CHAN), key=lambda d: -min(d, CHAN - d))
    barrier = pltpu.get_barrier_semaphore()
    for dx, dz in order:
        pl.semaphore_signal(barrier, inc=1, device_id=(peer(dx, dz), ch), device_id_type=MESH)
    for d in far_first:
        pl.semaphore_signal(barrier, inc=1, device_id=(me, lax.rem(ch + d, CHAN)), device_id_type=MESH)

    def block(j):
        return pl.ds(pl.multiple_of(j * CW, CW), CW)

    def channel_major(values, cb, dst):
        turned = jnp.transpose(values)
        for j in range(128 // CW):
            for h in range(PARTS):
                rows = slice(j * CW + h * CP, j * CW + h * CP + CP)
                both = jnp.concatenate([turned[rows, :BH], turned[rows, BH:]], axis=0)
                at = (cb * (128 // CW) + j) * CW
                dst[h, at : at + CW, :] = both.astype(bf16)

    loads[0].wait()
    loads[1].wait()
    for load in loads[3:]:
        load.start()
    for cb in range(CH // 128):
        lanes = slice(cb * 128, cb * 128 + 128)
        channel_major(k_ref[:, lanes].astype(f32) * v_ref[:, lanes].astype(f32), cb, prod_t)
    loads[2].wait()
    for g in range(8):
        taps_out[g] = taps_ref[g : g + 1, :].astype(f32)

    pl.semaphore_wait(barrier, SEQ - 1 + CHAN - 1)

    sends = []

    def exchange(src, dst, ssem, rsem):
        for dx, dz in order:
            j = peer(dx, dz)
            cp = pltpu.make_async_remote_copy(
                src.at[block(j)], dst.at[block(me)], ssem, rsem, device_id=(j, ch), device_id_type=MESH
            )
            cp.start()
            sends.append(cp)

    def arrived(dst, sem, count):
        pltpu.make_async_copy(dst.at[pl.ds(0, count)], dst.at[pl.ds(0, count)], sem).wait()

    exchange(prod_t.at[0], data_in.at[0], data_ssem.at[0], data_rsem.at[0])
    for dx, dz in order:
        j = peer(dx, dz)
        cp = pltpu.make_async_remote_copy(
            taps_out.at[j // 4], taps_in.at[me], taps_ssem, taps_rsem, device_id=(j, ch), device_id_type=MESH
        )
        cp.start()
        sends.append(cp)
    exchange(prod_t.at[1], data_in.at[1], data_ssem.at[1], data_rsem.at[1])
    taps_in[me] = taps_out[me // 4]
    for h in range(PARTS):
        data_in[h, block(me), :] = prod_t[h, block(me), :]

    loads[3].wait()
    for cb in range(CH // 128):
        lanes = slice(cb * 128, cb * 128 + 128)
        channel_major(q_ref[:, lanes].astype(f32), cb, q_t)

    for i in range(4, 8):
        loads[i].wait()
    arrived(taps_in, taps_rsem, SEQ - 1)
    for a in range(SEQ):
        taps_mat[a : a + 1, :] = taps_in[a]
    taps_y = jnp.dot(tfirst_ref[...], taps_mat[...].astype(bf16), preferred_element_type=f32)
    ty_re, ty_im = taps_y[:TPAD], taps_y[TPAD:]
    cos, sin = twid_ref[0], twid_ref[1]
    taps_spread = jnp.concatenate(
        [(ty_re * cos + ty_im * sin).astype(bf16), (ty_im * cos - ty_re * sin).astype(bf16)], axis=1
    )
    taps_spec[...] = jnp.dot(taps_spread, fwd[...], preferred_element_type=f32)
    loads[8].wait()
    loads[9].wait()

    zero = jnp.zeros((CP, BH), f32)

    def part(h):
        arrived(data_in.at[h], data_rsem.at[h], CH - CW)
        y = jnp.dot(first[...], data_in[h], preferred_element_type=f32)
        for bh in range(2):
            lanes = slice(bh * BH, bh * BH + BH)
            for m in range(ROWS // 16):
                res, ims = [], []
                for k1 in (2 * m, 2 * m + 1):
                    if k1 >= HALF:
                        res.append(zero)
                        ims.append(zero)
                        continue
                    at = k1 * CW + bh * CP
                    re = y[at : at + CP]
                    c = jnp.broadcast_to(twid_ref[0, k1 : k1 + 1, lanes], (CP, BH))
                    s = jnp.broadcast_to(twid_ref[1, k1 : k1 + 1, lanes], (CP, BH))
                    if 0 < k1 < HALF - 1:
                        at = (HALF + k1 - 1) * CW + bh * CP
                        im = y[at : at + CP]
                        res.append(re * c + im * s)
                        ims.append(im * c - re * s)
                    else:
                        res.append(re * c)
                        ims.append(-(re * s))
                rows = slice(m * 16, m * 16 + 16)
                spread[h, rows, lanes] = jnp.concatenate(res, axis=0).astype(bf16)
                spread[h, rows, slice(TOK + bh * BH, TOK + bh * BH + BH)] = jnp.concatenate(ims, axis=0).astype(bf16)

        for nb in range(TOK // 128):
            sp = jnp.dot(spread[h], fwd[:, nb * 256 : nb * 256 + 256], preferred_element_type=f32)
            lr, li = slice(nb * 256, nb * 256 + 128), slice(nb * 256 + 128, nb * 256 + 256)
            for m in range(ROWS // 16):
                res, ims = [], []
                for k1 in (2 * m, 2 * m + 1):
                    hr = jnp.broadcast_to(taps_spec[k1 : k1 + 1, lr], (CP, 128))
                    hi = jnp.broadcast_to(taps_spec[k1 : k1 + 1, li], (CP, 128))
                    rows = slice(k1 * CP, k1 * CP + CP)
                    sr, si = sp[rows, :128], sp[rows, 128:]
                    res.append(sr * hr - si * hi)
                    ims.append(sr * hi + si * hr)
                rows = slice(m * 16, m * 16 + 16)
                filtered[h, rows, lr] = jnp.concatenate(res, axis=0).astype(bf16)
                filtered[h, rows, li] = jnp.concatenate(ims, axis=0).astype(bf16)

        for nb in range(BH // 128):
            inv = jnp.dot(filtered[h], bwd[:, nb * 512 : nb * 512 + 512], preferred_element_type=f32)
            for k1 in range(HALF):
                rows = slice(k1 * CP, k1 * CP + CP)
                res, ims = [], []
                for bh in range(2):
                    lanes = slice(bh * BH + nb * 128, bh * BH + nb * 128 + 128)
                    c = jnp.broadcast_to(twid_ref[0, k1 : k1 + 1, lanes], (CP, 128))
                    s = jnp.broadcast_to(twid_ref[1, k1 : k1 + 1, lanes], (CP, 128))
                    re = inv[rows, bh * 256 : bh * 256 + 128]
                    im = inv[rows, bh * 256 + 128 : bh * 256 + 256]
                    res.append(re * c - im * s)
                    ims.append(im * c + re * s)
                lanes = slice(nb * 128, nb * 128 + 128)
                returned[h, k1 * CW : k1 * CW + CW, lanes] = jnp.concatenate(res, axis=0).astype(bf16)
                if 0 < k1 < HALF - 1:
                    at = (HALF + k1 - 1) * CW
                    returned[h, at : at + CW, lanes] = jnp.concatenate(ims, axis=0).astype(bf16)

        z = jnp.dot(last[...], returned[h], preferred_element_type=f32)
        back_out[h] = (z * (1.0 / N)).astype(bf16)
        exchange(back_out.at[h], back_in.at[h], back_ssem.at[h], back_rsem.at[h])
        back_in[h, block(me), :] = back_out[h, block(me), :]

    for h in range(PARTS):
        part(h)

    totals = [jnp.zeros((CP, BH), f32), jnp.zeros((CP, BH), f32)]
    for h in range(PARTS):
        arrived(back_in.at[h], back_rsem.at[h], CH - CW)
        for j in range(SEQ):
            rows = slice(j * CW, j * CW + CW)
            g = q_t[h, rows, :].astype(f32) * back_in[h, rows, :].astype(f32)
            g = g * g
            totals = [totals[0] + g[:CP], totals[1] + g[CP:]]
    sums = [jnp.sum(t, axis=0, keepdims=True) for t in totals]
    sums_out[...] = jnp.zeros((8, 128), f32)
    for i in range(TOK // 128):
        at = i * 128 % BH
        sums_out[i : i + 1, :] = sums[i * 128 // BH][:, at : at + 128]
    for d in far_first:
        cp = pltpu.make_async_remote_copy(
            sums_out, sums_in.at[ch], sum_ssem, sum_rsem, device_id=(me, lax.rem(ch + d, CHAN)), device_id_type=MESH
        )
        cp.start()
        sends.append(cp)
    sums_in[ch] = sums_out[...]

    for cb in range(CH // 128):
        rows = []
        for j in range(128 // CW):
            at = (cb * (128 // CW) + j) * CW
            for h in range(PARTS):
                tile = back_in[h, at : at + CW, :].astype(f32)
                rows.append(jnp.concatenate([tile[:CP], tile[CP:]], axis=1))
        conv_ref[:, cb * 128 : cb * 128 + 128] = jnp.transpose(jnp.concatenate(rows, axis=0)).astype(bf16)

    arrived(sums_in, sum_rsem, CHAN - 1)
    square = sums_in[0]
    for i in range(1, CHAN):
        square = square + sums_in[i]
    inverse = lax.rsqrt(square / D + NORM_EPS)
    for i in range(TOK // 128):
        rows = slice(i * 128, i * 128 + 128)
        inverse_ref[rows, :] = jnp.transpose(jnp.broadcast_to(inverse[i : i + 1, :], (128, 128)))
    for cp in sends:
        cp.wait_send()


def gate_and_norm(q_ref, conv_ref, inverse_ref, gain_ref, gated_ref, normed_ref):
    f32, bf16 = jnp.float32, jnp.bfloat16
    tokens = gated_ref.shape[0]
    rows = pl.ds(pl.multiple_of(pl.program_id(0) * tokens, tokens), tokens)
    inverse = inverse_ref[rows, :]
    for cb in range(CH // 128):
        lanes = slice(cb * 128, cb * 128 + 128)
        g = q_ref[rows, lanes].astype(f32) * conv_ref[rows, lanes].astype(f32)
        gated_ref[:, lanes] = g.astype(bf16)
        normed_ref[:, lanes] = (g * inverse * gain_ref[:, lanes]).astype(bf16)


def body(query_gate, key_gate, value_input, filter_taps, norm_gain):
    bf16, f32 = jnp.bfloat16, jnp.float32
    tables = [jnp.asarray(t) for t in constant_tables()]
    hbm = pl.BlockSpec(memory_space=pltpu.HBM)
    dma = pltpu.SemaphoreType.DMA
    operands = [query_gate, key_gate, value_input, jnp.transpose(filter_taps), *tables]
    vmem = pl.BlockSpec(memory_space=pltpu.VMEM)
    conv, inverse = pl.pallas_call(
        kernel,
        out_shape=[pltpu.VMEM((TOK, CH), bf16), pltpu.VMEM((TOK, 128), f32)],
        in_specs=[hbm] * 10,
        out_specs=[vmem, vmem],
        scratch_shapes=[
            pltpu.VMEM((TOK, CH), bf16),
            pltpu.VMEM((TOK, CH), bf16),
            pltpu.VMEM((TOK, CH), bf16),
            pltpu.VMEM((8, TOK), bf16),
            pltpu.VMEM((2 * TPAD, SEQ), bf16),
            pltpu.VMEM((2, TPAD, TOK), f32),
            pltpu.VMEM((PARTS, CH, BH), bf16),
            pltpu.VMEM((PARTS, CH, BH), bf16),
            pltpu.VMEM((8, 1, TOK), f32),
            pltpu.VMEM((SEQ, 1, TOK), f32),
            pltpu.VMEM((SEQ, TOK), f32),
            pltpu.VMEM((TPAD, 2 * TOK), f32),
            pltpu.VMEM((PARTS, CH, BH), bf16),
            pltpu.VMEM((FULL, CH), bf16),
            pltpu.VMEM((CH, FULL), bf16),
            pltpu.VMEM((2 * TOK, 2 * TOK), bf16),
            pltpu.VMEM((2 * TOK, 2 * TOK), bf16),
            pltpu.VMEM((PARTS, ROWS, 2 * TOK), bf16),
            pltpu.VMEM((PARTS, ROWS, 2 * TOK), bf16),
            pltpu.VMEM((PARTS, FULL, BH), bf16),
            pltpu.VMEM((PARTS, CH, BH), bf16),
            pltpu.VMEM((PARTS, CH, BH), bf16),
            pltpu.VMEM((8, 128), f32),
            pltpu.VMEM((CHAN, 8, 128), f32),
            dma((10,)), dma((PARTS,)), dma((PARTS,)), dma, dma, dma((PARTS,)), dma((PARTS,)), dma, dma,
        ],
        compiler_params=pltpu.CompilerParams(
            collective_id=0, has_side_effects=True, vmem_limit_bytes=48 * 1024 * 1024
        ),
    )(*[pltpu.with_memory_space_constraint(x, pltpu.HBM) for x in operands])
    steps = 2
    wide = pl.BlockSpec((TOK // steps, CH), lambda i: (i, 0))
    return pl.pallas_call(
        gate_and_norm,
        grid=(steps,),
        out_shape=[jax.ShapeDtypeStruct((TOK, CH), bf16)] * 2,
        in_specs=[vmem] * 4,
        out_specs=[wide, wide],
        compiler_params=pltpu.CompilerParams(vmem_limit_bytes=32 * 1024 * 1024),
    )(query_gate, conv, inverse, norm_gain.reshape(1, CH))


def solution(mesh):
    placed = (P("seq", "chan"), P("seq", "chan"), P("seq", "chan"), P("seq", "chan"), P("chan"))
    return jax.shard_map(
        body,
        mesh=mesh,
        in_specs=placed,
        out_specs=(P("seq", "chan"), P("seq", "chan")),
        check_vma=False,
    )
```
